1024 devices in a mesh: seabed: 64 (over x, z_lo, core), freq: 16 (over y, z_hi).
Axes of the slice: x: 8, y: 8, z: 8 (z_hi: 2, z_lo: 4; z = z_hi * 4 + z_lo), core: 2. Of those that a mesh axis runs over, the one named last changes fastest.
Arguments:
- uplift: bfloat16 [128, 32, 320, 128], P('freq', None, 'seabed'), may hold values from -6 to 6
- coefficient: float32 [320, 128], P('seabed'), may hold values from 0.06 to 0.24
- transfer: float32 [16, 2, 600, 40960], P('freq', None, None, 'seabed'), may hold values from -0.01953125 to 0.01953125
Outputs:
- sensors: float32 [128, 16, 2, 600], P('seabed', 'freq')
The draws below stay inside these ranges and needn't reach their ends.
All inputs are finite; a program needn't handle non-finite values.
Results may differ from the reference program's by a relative error of at most 0.0003.
Values sent between devices are 32-bit elements; how exact they have to be, the bound alone decides.
A program may use at most 32 MiB of HBM per device.

```python
import math
import jax
import jax.numpy as jnp
from jax import lax

PATCH = 128
SENS = 600
NV = 128
PASSES = 3
NT = 32
NF = 16
NR = 320


def block_scale(own_key, extent, cuts, low, high):
    def one(axis_at, shards_of):
        heights = jax.random.uniform(jax.random.fold_in(jax.random.fold_in(own_key, 6), axis_at), (shards_of,), jnp.float32, low / len(cuts), high / len(cuts))
        return jnp.repeat(jnp.exp(heights), extent[axis_at] // shards_of).reshape((-1,) + (1,) * (len(extent) - axis_at - 1))

    gain = one(*cuts[0])
    for cut in cuts[1:]:
        gain = gain * one(*cut)
    return gain


def bell_draw(rng, extent, spread, most, split=(), kind=jnp.bfloat16):
    gain = block_scale(rng, extent, split, -0.22, 0.18) if split else 1.0
    values = jax.random.normal(rng, extent, jnp.float32) * spread * gain
    return jnp.minimum(jnp.maximum(values, -most), most).astype(kind)


def setup_inputs(seed: int = 0) -> dict:
    key_of = jax.random.split(jax.random.key(seed), 4)
    return {
        "uplift": bell_draw(key_of[0], (NV, NT, NR, PATCH), 1.0, 6.0, ((0, 16), (2, 64))),
        "coefficient": jnp.clip(jnp.exp(math.log(0.24) - 1.3862944 * jax.random.uniform(key_of[1], (NR, PATCH), jnp.float32) ** block_scale(key_of[1], (NR, PATCH), ((0, 64),), -0.2, 0.2)), 0.06, 0.24),
        "transfer": bell_draw(key_of[2], (NF, 2, SENS, NR * PATCH), (2 * NR * PATCH) ** -0.5, 0.01953125, ((0, 16), (3, 64)), jnp.float32),
    }


def dft_table(steps_count, freq_count):
    times = jnp.arange(steps_count, dtype=jnp.int32)
    freqs = jnp.arange(freq_count, dtype=jnp.int32)
    phase = (freqs[:, None] * times[None, :] % steps_count).astype(jnp.float32) * (2.0 * math.pi / steps_count)
    scale = 1.0 / math.sqrt(steps_count)
    return jnp.stack([jnp.cos(phase), -jnp.sin(phase)], 1).reshape(2 * freq_count, steps_count) * scale

def smooth(field, coefficient):
    padded = jnp.pad(field, ((0, 0), (1, 1), (1, 1)))
    beside = padded[:, 2:, 1:-1] + padded[:, :-2, 1:-1] + padded[:, 1:-1, 2:] + padded[:, 1:-1, :-2]
    return field + coefficient * (beside - 4.0 * field)

def reference(uplift, coefficient, transfer):
    table = dft_table(NT, NF)

    def one_vector(series):
        field = series.astype(jnp.float32)
        for step in range(PASSES):
            field = smooth(field, coefficient)
        flat = field.reshape(NT, NR * PATCH)
        return jnp.dot(table, flat, precision=lax.Precision.HIGHEST).reshape(NF, 2, NR * PATCH)
    spectra = lax.map(one_vector, uplift)
    by_freq = jnp.transpose(spectra, (1, 0, 2, 3))

    def one_freq(pair):
        spectrum, block = pair
        products = jnp.einsum('vbc,asc->vbas', spectrum, block, precision=lax.Precision.HIGHEST)
        real_part = products[:, 0, 0] - products[:, 1, 1]
        imag_part = products[:, 1, 0] + products[:, 0, 1]
        return jnp.stack([real_part, imag_part], 1)
    result = lax.map(one_freq, (by_freq, transfer))
    return jnp.transpose(result, (1, 0, 2, 3))
```

```python
import functools
import math

import jax
import jax.numpy as jnp
import numpy as np
from jax import lax
from jax.experimental import pallas as pl
from jax.experimental.pallas import tpu as pltpu
from jax.sharding import PartitionSpec as P

MESH = pl.DeviceIdType.MESH
PASSES = 3
CORES = 2
Z = 4
GROUPS = 4
F32 = jnp.float32
BF16 = jnp.bfloat16


def split(value):
    high = value.astype(BF16)
    return high, (value - high.astype(F32)).astype(BF16)


def dot_nt(a, b):
    return lax.dot_general(a, b, (((1,), (1,)), ((), ())), preferred_element_type=F32)


def block_table(vectors, steps, freqs):
    phase = (np.arange(freqs)[:, None] * np.arange(steps)[None, :] % steps) * (2.0 * math.pi / steps)
    table = np.stack([np.cos(phase), -np.sin(phase)], 1) / math.sqrt(steps)
    wide = np.einsum("kbt,vw->kbvwt", table, np.eye(vectors))
    wide = wide.reshape(2 * freqs * vectors, vectors * steps).astype(np.float32)
    high = wide.astype(BF16)
    low = (wide - high.astype(np.float32)).astype(BF16)
    return np.stack([high, low])


def kernel(
    dims, x_ref, coef_ref, table_ref, transfer_ref, out_ref,
    ext, coefs, outgoing, incoming, raw, t_high, t_low, l_high, l_low, prod, pair, x_out, x_in, z_out, z_in,
    raw_sem, coef_sems, halo_send, halo_recv, a2a_send, a2a_recv, pair_sems, x_send, x_recv, z_send, z_recv,
):
    X, F, vectors, steps, rows, width, sens, sens_pad = dims
    size = F // GROUPS
    strips = X * Z * CORES
    span = Z * CORES * 2
    s = lax.axis_index("seabed")
    f = lax.axis_index("freq")
    core = s % CORES
    z = (s // CORES) % Z
    x = s // (CORES * Z)
    group_at = x * (CORES * Z)
    local = s % (CORES * Z)
    has_low = s > 0
    has_high = s < strips - 1
    crosses_low = (local == 0) & has_low
    crosses_high = (local == CORES * Z - 1) & has_high

    def x_peer(step):
        return (x + step) % X

    def x_device(at):
        return ((at * Z + z) * CORES + core, f)

    def z_device(at):
        return (group_at + at, f)

    fetch = [pltpu.make_async_copy(transfer_ref.at[0, a], raw.at[a, pl.ds(0, sens)], raw_sem.at[a]) for a in range(2)]
    for copy in fetch:
        copy.start()

    barrier = pltpu.get_barrier_semaphore()

    @pl.loop(1, F)
    def _(step):
        pl.semaphore_signal(barrier, inc=1, device_id=(s, (f + step) % F), device_id_type=MESH)

    @pl.loop(1, X)
    def _(step):
        pl.semaphore_signal(barrier, inc=1, device_id=x_device(x_peer(step)), device_id_type=MESH)

    @pl.loop(1, CORES * Z)
    def _(step):
        pl.semaphore_signal(barrier, inc=1, device_id=z_device((local + step) % (CORES * Z)), device_id_type=MESH)

    @pl.when(crosses_low)
    def _():
        pl.semaphore_signal(barrier, inc=1, device_id=(s - 1, f), device_id_type=MESH)

    @pl.when(crosses_high)
    def _():
        pl.semaphore_signal(barrier, inc=1, device_id=(s + 1, f), device_id_type=MESH)

    for r in range(rows):
        block = x_ref[:, r].reshape(vectors * steps, width)
        ext[PASSES + r] = jnp.dot(table_ref[0], block, preferred_element_type=F32) + jnp.dot(
            table_ref[1], block, preferred_element_type=F32
        )
        coefs[PASSES + r] = jnp.broadcast_to(coef_ref[pl.ds(r, 1), :], (8, width))
    raw[:, pl.ds(sens, sens_pad - sens)] = jnp.zeros((2, sens_pad - sens, raw.shape[2]), F32)

    peers = (F - 1) + (X - 1) + (CORES * Z - 1)
    crosses = crosses_low | crosses_high

    @pl.when(crosses)
    def _():
        pl.semaphore_wait(barrier, peers + 1)

    @pl.when(jnp.logical_not(crosses))
    def _():
        pl.semaphore_wait(barrier, peers)

    lines = 2 * vectors
    LOW, HIGH = 0, 1

    def block_of(g):
        return (f // size + g) % GROUPS

    def coef_copy(side):
        source = coefs.at[pl.ds(rows, PASSES)] if side == LOW else coefs.at[pl.ds(PASSES, PASSES)]
        target = coefs.at[pl.ds(0, PASSES)] if side == LOW else coefs.at[pl.ds(PASSES + rows, PASSES)]
        peer = s + 1 if side == LOW else s - 1
        return pltpu.make_async_remote_copy(
            src_ref=source, dst_ref=target, send_sem=coef_sems.at[side], recv_sem=coef_sems.at[2 + side],
            device_id=(peer, f), device_id_type=MESH,
        )

    def halo_copy(side, g):
        at = pl.ds(pl.multiple_of(block_of(g) * (size * lines), size * lines), size * lines)
        source = ext.at[pl.ds(rows, PASSES), at] if side == LOW else ext.at[pl.ds(PASSES, PASSES), at]
        target = ext.at[pl.ds(0, PASSES), at] if side == LOW else ext.at[pl.ds(PASSES + rows, PASSES), at]
        peer = s + 1 if side == LOW else s - 1
        return pltpu.make_async_remote_copy(
            src_ref=source, dst_ref=target, send_sem=halo_send.at[side, g], recv_sem=halo_recv.at[side, g],
            device_id=(peer, f), device_id_type=MESH,
        )

    @pl.when(has_high)
    def _():
        coef_copy(LOW).start()
        halo_copy(LOW, 0).start()

    @pl.when(has_low)
    def _():
        coef_copy(HIGH).start()
        halo_copy(HIGH, 0).start()

    @pl.loop(1, GROUPS)
    def _(g):
        @pl.when(has_high)
        def _():
            halo_copy(LOW, g).start()

        @pl.when(has_low)
        def _():
            halo_copy(HIGH, g).start()

    @pl.when(jnp.logical_not(has_low))
    def _():
        ext[pl.ds(0, PASSES)] = jnp.zeros((PASSES,) + ext.shape[1:], F32)
        coefs[pl.ds(0, PASSES)] = jnp.zeros((PASSES, 8, width), F32)

    @pl.when(jnp.logical_not(has_high))
    def _():
        ext[pl.ds(PASSES + rows, PASSES)] = jnp.zeros((PASSES,) + ext.shape[1:], F32)
        coefs[pl.ds(PASSES + rows, PASSES)] = jnp.zeros((PASSES, 8, width), F32)

    for copy in fetch:
        copy.wait()
    cells = rows * width
    part = 32

    @pl.loop(0, sens_pad // part)
    def _(i):
        at = pl.ds(pl.multiple_of(i * part, part), part)
        for a in range(2):
            high, low = split(raw[a, at])
            t_high[at, pl.ds(a * cells, cells)] = high
            t_low[at, pl.ds(a * cells, cells)] = low

    @pl.when(has_low)
    def _():
        coef_copy(LOW).wait_recv()

    @pl.when(has_high)
    def _():
        coef_copy(HIGH).wait_recv()

    lane = lax.broadcasted_iota(jnp.int32, (8, width), 1)

    def smoothed(at):
        u = [ext[r, at] for r in range(rows + 2 * PASSES)]
        for p in range(PASSES):
            later = []
            for r in range(1, len(u) - 1):
                left = jnp.where(lane == 0, 0.0, pltpu.roll(u[r], 1, 1))
                right = jnp.where(lane == width - 1, 0.0, pltpu.roll(u[r], width - 1, 1))
                beside = (u[r + 1] + u[r - 1]) + (left + right)
                later.append(u[r] + coefs[r + p] * (beside - 4.0 * u[r]))
            u = later
        return u

    def a2a_copy(k, source):
        return pltpu.make_async_remote_copy(
            src_ref=outgoing.at[k], dst_ref=incoming.at[source], send_sem=a2a_send.at[k], recv_sem=a2a_recv.at[source],
            device_id=(s, k), device_id_type=MESH,
        )

    @pl.loop(0, GROUPS)
    def _(g):
        @pl.when(has_low)
        def _():
            halo_copy(LOW, g).wait_recv()

        @pl.when(has_high)
        def _():
            halo_copy(HIGH, g).wait_recv()

        @pl.loop(0, size)
        def _(j):
            k = block_of(g) * size + (f + j) % size
            for b in range(2):
                at = pl.ds(pl.multiple_of(k * lines + b * vectors, 8), 8)
                for r, value in enumerate(smoothed(at)):
                    outgoing[k, b, r] = value

            @pl.when(k != f)
            def _():
                a2a_copy(k, f).start()

    width_all = rows * width

    @pl.loop(0, F // 2)
    def _(q):
        for own in range(2):
            at = q * 2 + own

            @pl.when(at != f)
            def _():
                pltpu.make_async_remote_copy(
                    src_ref=outgoing.at[at], dst_ref=incoming.at[at], send_sem=a2a_send.at[at],
                    recv_sem=a2a_recv.at[at], device_id=(s, at), device_id_type=MESH,
                ).wait_recv()

            @pl.when(at == f)
            def _():
                incoming[f] = outgoing[f]

        here = pl.ds(pl.multiple_of(q * 16, 16), 16)
        for r in range(rows):
            real = split(incoming[pl.ds(q * 2, 2), 0, r].reshape(16, width))
            imag = split(incoming[pl.ds(q * 2, 2), 1, r].reshape(16, width))
            for store, re, im in ((l_high, real[0], imag[0]), (l_low, real[1], imag[1])):
                store[0, here, pl.ds(r * width, width)] = re
                store[0, here, pl.ds(width_all + r * width, width)] = -im
                store[1, here, pl.ds(r * width, width)] = im
                store[1, here, pl.ds(width_all + r * width, width)] = re

    def products(part_at):
        for first in range(0, sens_pad, 256):
            count = min(256, sens_pad - first)
            at = pl.ds(first, count)
            total = dot_nt(l_high[part_at], t_high[at])
            total += dot_nt(l_low[part_at], t_high[at])
            total += dot_nt(l_high[part_at], t_low[at])
            prod[part_at, :, at] = total

    other = 1 - core
    products(other)
    pair_copy = pltpu.make_async_remote_copy(
        src_ref=prod.at[other], dst_ref=pair, send_sem=pair_sems.at[0], recv_sem=pair_sems.at[1],
        device_id=(group_at + z * CORES + other, f), device_id_type=MESH,
    )
    pair_copy.start()
    products(core)
    pair_copy.wait_recv()

    def x_copy(to, source):
        return pltpu.make_async_remote_copy(
            src_ref=x_out.at[to], dst_ref=x_in.at[source], send_sem=x_send.at[to], recv_sem=x_recv.at[source],
            device_id=x_device(to), device_id_type=MESH,
        )

    @pl.loop(0, X)
    def _(step):
        to = x_peer(step + 1)
        at = pl.ds(pl.multiple_of(to * span, span), span)
        x_out[to] = prod[core, at] + pair[at]

        @pl.when(to != x)
        def _():
            x_copy(to, x).start()

    total = x_out[x]
    for step in range(1, X):
        source = x_peer(step)
        pltpu.make_async_remote_copy(
            src_ref=x_out.at[source], dst_ref=x_in.at[source], send_sem=x_send.at[source], recv_sem=x_recv.at[source],
            device_id=x_device(source), device_id_type=MESH,
        ).wait_recv()
        total += x_in[source]
    for at in range(CORES * Z):
        z_out[at] = total[2 * at : 2 * at + 2]

    def z_copy(to, source):
        return pltpu.make_async_remote_copy(
            src_ref=z_out.at[to], dst_ref=z_in.at[source], send_sem=z_send.at[to], recv_sem=z_recv.at[source],
            device_id=z_device(to), device_id_type=MESH,
        )

    @pl.loop(1, CORES * Z)
    def _(step):
        z_copy((local + step) % (CORES * Z), local).start()

    z_in[local] = z_out[local]

    @pl.loop(1, CORES * Z)
    def _(step):
        source = (local + step) % (CORES * Z)
        z_copy(source, source).wait_recv()

    for part_at in range(2):
        result = z_in[part_at]
        for at in range(1, Z):
            result += z_in[at * CORES + part_at]
        for v in range(2):
            out_ref[v, 0, pl.ds(part_at, 1)] = result[v : v + 1, :sens]

    @pl.when(has_high)
    def _():
        coef_copy(LOW).wait_send()

    @pl.when(has_low)
    def _():
        coef_copy(HIGH).wait_send()

    @pl.loop(0, GROUPS)
    def _(g):
        @pl.when(has_high)
        def _():
            halo_copy(LOW, g).wait_send()

        @pl.when(has_low)
        def _():
            halo_copy(HIGH, g).wait_send()

    @pl.loop(1, F)
    def _(step):
        a2a_copy((f + step) % F, f).wait_send()

    pair_copy.wait_send()

    @pl.loop(1, X)
    def _(step):
        x_copy(x_peer(step), x).wait_send()

    @pl.loop(1, CORES * Z)
    def _(step):
        z_copy((local + step) % (CORES * Z), local).wait_send()


def shards(uplift, coefficient, transfer):
    vectors, steps, rows, width = uplift.shape
    sens = transfer.shape[2]
    F = lax.axis_size("freq")
    strips = lax.axis_size("seabed")
    X = strips // (Z * CORES)
    all_vectors = vectors * F
    span = Z * CORES * 2
    sens_pad = -(-sens // 128) * 128
    cells = rows * width
    dims = (X, F, vectors, steps, rows, width, sens, sens_pad)
    table = jnp.asarray(block_table(vectors, steps, F))
    field = jnp.transpose(uplift, (0, 2, 1, 3))
    dma = pltpu.SemaphoreType.DMA
    vmem = pl.BlockSpec(memory_space=pltpu.VMEM)
    return pl.pallas_call(
        functools.partial(kernel, dims),
        out_shape=jax.ShapeDtypeStruct((2, 1, 2, sens), F32),
        in_specs=[vmem, vmem, vmem, pl.BlockSpec(memory_space=pl.ANY)],
        out_specs=vmem,
        scratch_shapes=[
            pltpu.VMEM((rows + 2 * PASSES, 2 * F * vectors, width), F32),
            pltpu.VMEM((rows + 2 * PASSES, 8, width), F32),
            pltpu.VMEM((F, 2, rows, vectors, width), F32),
            pltpu.VMEM((F, 2, rows, vectors, width), F32),
            pltpu.VMEM((2, sens_pad, cells), F32),
            pltpu.VMEM((sens_pad, 2 * cells), BF16),
            pltpu.VMEM((sens_pad, 2 * cells), BF16),
            pltpu.VMEM((2, all_vectors, 2 * cells), BF16),
            pltpu.VMEM((2, all_vectors, 2 * cells), BF16),
            pltpu.VMEM((2, all_vectors, sens_pad), F32),
            pltpu.VMEM((all_vectors, sens_pad), F32),
            pltpu.VMEM((X, span, sens_pad), F32),
            pltpu.VMEM((X, span, sens_pad), F32),
            pltpu.VMEM((CORES * Z, 2, sens_pad), F32),
            pltpu.VMEM((CORES * Z, 2, sens_pad), F32),
            dma((2,)),
            dma((4,)),
            dma((2, GROUPS)),
            dma((2, GROUPS)),
            dma((F,)),
            dma((F,)),
            dma((2,)),
            dma((X,)),
            dma((X,)),
            dma((CORES * Z,)),
            dma((CORES * Z,)),
        ],
        compiler_params=pltpu.CompilerParams(
            collective_id=0, has_side_effects=True, vmem_limit_bytes=40 * 1024 * 1024
        ),
    )(field, coefficient, table, transfer)


def solution(mesh):
    placed = (P("freq", None, "seabed", None), P("seabed", None), P("freq", None, None, "seabed"))
    return jax.shard_map(
        shards,
        mesh=mesh,
        in_specs=placed,
        out_specs=P("seabed", "freq", None, None),
        check_vma=False,
    )
```

```python
import functools
import math

import jax
import jax.numpy as jnp
import numpy as np
from jax import lax
from jax.experimental import pallas as pl
from jax.experimental.pallas import tpu as pltpu
from jax.sharding import PartitionSpec as P

MESH = pl.DeviceIdType.MESH
PASSES = 3
CORES = 2
Z = 4
GROUPS = 4
AHEAD = 2
F32 = jnp.float32
BF16 = jnp.bfloat16


def split(value):
    high = value.astype(BF16)
    return high, (value - high.astype(F32)).astype(BF16)


def dot_nt(a, b):
    return lax.dot_general(a, b, (((1,), (1,)), ((), ())), preferred_element_type=F32)


def block_table(vectors, steps, freqs):
    phase = (np.arange(freqs)[:, None] * np.arange(steps)[None, :] % steps) * (2.0 * math.pi / steps)
    table = np.stack([np.cos(phase), -np.sin(phase)], 1) / math.sqrt(steps)
    wide = np.einsum("kbt,vw->kbvwt", table, np.eye(vectors))
    wide = wide.reshape(2 * freqs * vectors, vectors * steps).astype(np.float32)
    high = wide.astype(BF16)
    low = (wide - high.astype(np.float32)).astype(BF16)
    return np.stack([high, low])


def kernel(
    dims, x_hbm, coef_hbm, table_hbm, transfer_ref, out_ref,
    x_ref, coef_ref, table_ref, ext, coefs, outgoing, incoming, raw, t_high, t_low, parts, prod, pair, x_out, x_in, z_out, z_in,
    in_sems, raw_sem, coef_sems, halo_send, halo_recv, a2a_send, a2a_recv, pair_send, pair_recv, x_send, x_recv, z_send, z_recv,
):
    X, F, vectors, steps, rows, width, sens, sens_pad = dims
    size = F // GROUPS
    block_rows = size * vectors
    strips = X * Z * CORES
    span = Z * CORES * 2
    s = lax.axis_index("seabed")
    f = lax.axis_index("freq")
    core = s % CORES
    z = (s // CORES) % Z
    x = s // (CORES * Z)
    group_at = x * (CORES * Z)
    local = s % (CORES * Z)
    has_low = s > 0
    has_high = s < strips - 1
    crosses_low = (local == 0) & has_low
    crosses_high = (local == CORES * Z - 1) & has_high

    def x_peer(step):
        return (x + step) % X

    def x_device(at):
        return ((at * Z + z) * CORES + core, f)

    def z_device(at):
        return (group_at + at, f)

    first = [
        pltpu.make_async_copy(source, target, in_sems.at[i])
        for i, (source, target) in enumerate(((x_hbm, x_ref), (table_hbm, table_ref), (coef_hbm, coef_ref)))
    ]
    for copy in first:
        copy.start()
    fetch = [pltpu.make_async_copy(transfer_ref.at[0, a], raw.at[a, pl.ds(0, sens)], raw_sem.at[a]) for a in range(2)]

    barrier = pltpu.get_barrier_semaphore()

    @pl.when(crosses_low)
    def _():
        pl.semaphore_signal(barrier, inc=1, device_id=(s - 1, f), device_id_type=MESH)

    @pl.when(crosses_high)
    def _():
        pl.semaphore_signal(barrier, inc=1, device_id=(s + 1, f), device_id_type=MESH)

    @pl.loop(1, F)
    def _(step):
        pl.semaphore_signal(barrier, inc=1, device_id=(s, (f + step) % F), device_id_type=MESH)

    @pl.loop(1, X)
    def _(step):
        pl.semaphore_signal(barrier, inc=1, device_id=x_device(x_peer(step)), device_id_type=MESH)

    @pl.loop(1, CORES * Z)
    def _(step):
        pl.semaphore_signal(barrier, inc=1, device_id=z_device((local + step) % (CORES * Z)), device_id_type=MESH)

    for copy in fetch:
        copy.start()
    for copy in first:
        copy.wait()

    for r in range(rows):
        block = x_ref[:, r].reshape(vectors * steps, width)
        ext[PASSES + r] = jnp.dot(table_ref[0], block, preferred_element_type=F32) + jnp.dot(
            table_ref[1], block, preferred_element_type=F32
        )
        coefs[PASSES + r] = jnp.broadcast_to(coef_ref[pl.ds(r, 1), :], (8, width))
    raw[:, pl.ds(sens, sens_pad - sens)] = jnp.zeros((2, sens_pad - sens, raw.shape[2]), F32)

    peers = (F - 1) + (X - 1) + (CORES * Z - 1)
    crosses = crosses_low | crosses_high

    @pl.when(crosses)
    def _():
        pl.semaphore_wait(barrier, peers + 1)

    @pl.when(jnp.logical_not(crosses))
    def _():
        pl.semaphore_wait(barrier, peers)

    lines = 2 * vectors
    LOW, HIGH = 0, 1

    def block_of(g, x_at):
        return (f // size + g + x_at * GROUPS // X) % GROUPS

    def coef_copy(side):
        source = coefs.at[pl.ds(rows, PASSES)] if side == LOW else coefs.at[pl.ds(PASSES, PASSES)]
        target = coefs.at[pl.ds(0, PASSES)] if side == LOW else coefs.at[pl.ds(PASSES + rows, PASSES)]
        peer = s + 1 if side == LOW else s - 1
        return pltpu.make_async_remote_copy(
            src_ref=source, dst_ref=target, send_sem=coef_sems.at[side], recv_sem=coef_sems.at[2 + side],
            device_id=(peer, f), device_id_type=MESH,
        )

    def halo_copy(side, g, x_at):
        at = pl.ds(pl.multiple_of(block_of(g, x_at) * (size * lines), size * lines), size * lines)
        source = ext.at[pl.ds(rows, PASSES), at] if side == LOW else ext.at[pl.ds(PASSES, PASSES), at]
        target = ext.at[pl.ds(0, PASSES), at] if side == LOW else ext.at[pl.ds(PASSES + rows, PASSES), at]
        peer = s + 1 if side == LOW else s - 1
        return pltpu.make_async_remote_copy(
            src_ref=source, dst_ref=target, send_sem=halo_send.at[side, g], recv_sem=halo_recv.at[side, g],
            device_id=(peer, f), device_id_type=MESH,
        )

    def halo_start(g):
        @pl.when(has_high)
        def _():
            halo_copy(LOW, g, (s + 1) // (CORES * Z)).start()

        @pl.when(has_low)
        def _():
            halo_copy(HIGH, g, (s - 1) // (CORES * Z)).start()

    @pl.when(has_high)
    def _():
        coef_copy(LOW).start()

    @pl.when(has_low)
    def _():
        coef_copy(HIGH).start()

    for g in range(min(AHEAD, GROUPS)):
        halo_start(g)

    @pl.when(jnp.logical_not(has_low))
    def _():
        ext[pl.ds(0, PASSES)] = jnp.zeros((PASSES,) + ext.shape[1:], F32)
        coefs[pl.ds(0, PASSES)] = jnp.zeros((PASSES, 8, width), F32)

    @pl.when(jnp.logical_not(has_high))
    def _():
        ext[pl.ds(PASSES + rows, PASSES)] = jnp.zeros((PASSES,) + ext.shape[1:], F32)
        coefs[pl.ds(PASSES + rows, PASSES)] = jnp.zeros((PASSES, 8, width), F32)

    for copy in fetch:
        copy.wait()
    cells = rows * width
    part = 32

    @pl.loop(0, sens_pad // part)
    def _(i):
        at = pl.ds(pl.multiple_of(i * part, part), part)
        for a in range(2):
            high, low = split(raw[a, at])
            t_high[at, pl.ds(a * cells, cells)] = high
            t_low[at, pl.ds(a * cells, cells)] = low

    @pl.when(has_low)
    def _():
        coef_copy(LOW).wait_recv()

    @pl.when(has_high)
    def _():
        coef_copy(HIGH).wait_recv()

    lane = lax.broadcasted_iota(jnp.int32, (8, width), 1)

    def smoothed(at):
        u = [ext[r, at] for r in range(rows + 2 * PASSES)]
        for p in range(PASSES):
            later = []
            for r in range(1, len(u) - 1):
                left = jnp.where(lane == 0, 0.0, pltpu.roll(u[r], 1, 1))
                right = jnp.where(lane == width - 1, 0.0, pltpu.roll(u[r], width - 1, 1))
                beside = (u[r + 1] + u[r - 1]) + (left + right)
                later.append(u[r] + coefs[r + p] * (beside - 4.0 * u[r]))
            u = later
        return u

    def a2a_copy(k, source):
        return pltpu.make_async_remote_copy(
            src_ref=outgoing.at[k], dst_ref=incoming.at[source], send_sem=a2a_send.at[k], recv_sem=a2a_recv.at[source],
            device_id=(s, k), device_id_type=MESH,
        )

    @pl.loop(0, GROUPS)
    def _(g):
        @pl.when(has_low)
        def _():
            halo_copy(LOW, g, x).wait_recv()

        @pl.when(has_high)
        def _():
            halo_copy(HIGH, g, x).wait_recv()

        @pl.when(g + AHEAD < GROUPS)
        def _():
            halo_start(g + AHEAD)

        @pl.loop(0, size)
        def _(j):
            k = block_of(g, x) * size + (f + j) % size
            for b in range(2):
                at = pl.ds(pl.multiple_of(k * lines + b * vectors, 8), 8)
                for r, value in enumerate(smoothed(at)):
                    outgoing[k, b, r] = value

            @pl.when(k != f)
            def _():
                a2a_copy(k, f).start()

            @pl.when(k == f)
            def _():
                incoming[f] = outgoing[f]

    other = 1 - core

    def arrived(g):
        return (f // size + 2 * GROUPS - g - x * GROUPS // X) % GROUPS

    def rows_of(block):
        return pl.ds(pl.multiple_of(block * block_rows, block_rows), block_rows)

    def pair_copy(block):
        return pltpu.make_async_remote_copy(
            src_ref=prod.at[other, rows_of(block)], dst_ref=pair.at[rows_of(block)], send_sem=pair_send.at[block],
            recv_sem=pair_recv.at[block], device_id=(group_at + z * CORES + other, f), device_id_type=MESH,
        )

    def products(block):
        for j in range(size):
            at = block * size + j

            @pl.when(at != f)
            def _():
                pltpu.make_async_remote_copy(
                    src_ref=outgoing.at[at], dst_ref=incoming.at[at], send_sem=a2a_send.at[at],
                    recv_sem=a2a_recv.at[at], device_id=(s, at), device_id_type=MESH,
                ).wait_recv()

        for q in range(size // 2):
            here = pl.ds(q * 16, 16)
            for r in range(rows):
                real = split(incoming[pl.ds(block * size + q * 2, 2), 0, r].reshape(16, width))
                imag = split(incoming[pl.ds(block * size + q * 2, 2), 1, r].reshape(16, width))
                for i in range(2):
                    parts[i, 0, here, pl.ds(r * width, width)] = real[i]
                    parts[i, 0, here, pl.ds(cells + r * width, width)] = -imag[i]
                    parts[i, 1, here, pl.ds(r * width, width)] = imag[i]
                    parts[i, 1, here, pl.ds(cells + r * width, width)] = real[i]
        both = parts[...].reshape(4 * block_rows, 2 * cells)
        for first in range(0, sens_pad, 256):
            at = pl.ds(first, min(256, sens_pad - first))
            all_high = dot_nt(both, t_high[at])
            total = all_high[: 2 * block_rows] + all_high[2 * block_rows :]
            total += dot_nt(both[: 2 * block_rows], t_low[at])
            prod[0, rows_of(block), at] = total[:block_rows]
            prod[1, rows_of(block), at] = total[block_rows:]
        pair_copy(block).start()

    def x_copy(to, source):
        return pltpu.make_async_remote_copy(
            src_ref=x_out.at[to], dst_ref=x_in.at[source], send_sem=x_send.at[to], recv_sem=x_recv.at[source],
            device_id=x_device(to), device_id_type=MESH,
        )

    def pass_on(block):
        pair_copy(block).wait_recv()
        for i in range(block_rows // span):
            to = block * (block_rows // span) + i
            at = pl.ds(pl.multiple_of(to * span, span), span)
            x_out[to] = prod[core, at] + pair[at]

            @pl.when(to != x)
            def _():
                x_copy(to, x).start()

    @pl.loop(0, GROUPS)
    def _(g):
        products(arrived(g))

        @pl.when(g > 0)
        def _():
            pass_on(arrived(g - 1))

    pass_on(arrived(GROUPS - 1))

    total = x_out[x]
    for step in range(1, X):
        source = x_peer(step)
        pltpu.make_async_remote_copy(
            src_ref=x_out.at[source], dst_ref=x_in.at[source], send_sem=x_send.at[source], recv_sem=x_recv.at[source],
            device_id=x_device(source), device_id_type=MESH,
        ).wait_recv()
        total += x_in[source]
    for at in range(CORES * Z):
        z_out[at] = total[2 * at : 2 * at + 2]

    def z_copy(to, source):
        return pltpu.make_async_remote_copy(
            src_ref=z_out.at[to], dst_ref=z_in.at[source], send_sem=z_send.at[to], recv_sem=z_recv.at[source],
            device_id=z_device(to), device_id_type=MESH,
        )

    @pl.loop(1, CORES * Z)
    def _(step):
        z_copy((local + step) % (CORES * Z), local).start()

    z_in[local] = z_out[local]

    @pl.loop(1, CORES * Z)
    def _(step):
        source = (local + step) % (CORES * Z)
        z_copy(source, source).wait_recv()

    for part_at in range(2):
        result = z_in[part_at]
        for at in range(1, Z):
            result += z_in[at * CORES + part_at]
        for v in range(2):
            out_ref[v, 0, pl.ds(part_at, 1)] = result[v : v + 1, :sens]

    @pl.when(has_high)
    def _():
        coef_copy(LOW).wait_send()

    @pl.when(has_low)
    def _():
        coef_copy(HIGH).wait_send()

    @pl.loop(0, GROUPS)
    def _(g):
        @pl.when(has_high)
        def _():
            halo_copy(LOW, g, (s + 1) // (CORES * Z)).wait_send()

        @pl.when(has_low)
        def _():
            halo_copy(HIGH, g, (s - 1) // (CORES * Z)).wait_send()

    @pl.loop(1, F)
    def _(step):
        a2a_copy((f + step) % F, f).wait_send()

    @pl.loop(0, GROUPS)
    def _(block):
        pair_copy(block).wait_send()

    @pl.loop(1, X)
    def _(step):
        x_copy(x_peer(step), x).wait_send()

    @pl.loop(1, CORES * Z)
    def _(step):
        z_copy((local + step) % (CORES * Z), local).wait_send()


def shards(uplift, coefficient, transfer):
    vectors, steps, rows, width = uplift.shape
    sens = transfer.shape[2]
    F = lax.axis_size("freq")
    strips = lax.axis_size("seabed")
    X = strips // (Z * CORES)
    all_vectors = vectors * F
    span = Z * CORES * 2
    sens_pad = -(-sens // 128) * 128
    cells = rows * width
    dims = (X, F, vectors, steps, rows, width, sens, sens_pad)
    table = jnp.asarray(block_table(vectors, steps, F))
    field = jnp.transpose(uplift, (0, 2, 1, 3))
    dma = pltpu.SemaphoreType.DMA
    vmem = pl.BlockSpec(memory_space=pltpu.VMEM)
    return pl.pallas_call(
        functools.partial(kernel, dims),
        out_shape=jax.ShapeDtypeStruct((2, 1, 2, sens), F32),
        in_specs=[pl.BlockSpec(memory_space=pltpu.HBM)] * 4,
        out_specs=vmem,
        scratch_shapes=[
            pltpu.VMEM((vectors, rows, steps, width), BF16),
            pltpu.VMEM((rows, width), F32),
            pltpu.VMEM(table.shape, BF16),
            pltpu.VMEM((rows + 2 * PASSES, 2 * F * vectors, width), F32),
            pltpu.VMEM((rows + 2 * PASSES, 8, width), F32),
            pltpu.VMEM((F, 2, rows, vectors, width), F32),
            pltpu.VMEM((F, 2, rows, vectors, width), F32),
            pltpu.VMEM((2, sens_pad, cells), F32),
            pltpu.VMEM((sens_pad, 2 * cells), BF16),
            pltpu.VMEM((sens_pad, 2 * cells), BF16),
            pltpu.VMEM((2, 2, all_vectors // GROUPS, 2 * cells), BF16),
            pltpu.VMEM((2, all_vectors, sens_pad), F32),
            pltpu.VMEM((all_vectors, sens_pad), F32),
            pltpu.VMEM((X, span, sens_pad), F32),
            pltpu.VMEM((X, span, sens_pad), F32),
            pltpu.VMEM((CORES * Z, 2, sens_pad), F32),
            pltpu.VMEM((CORES * Z, 2, sens_pad), F32),
            dma((3,)),
            dma((2,)),
            dma((4,)),
            dma((2, GROUPS)),
            dma((2, GROUPS)),
            dma((F,)),
            dma((F,)),
            dma((GROUPS,)),
            dma((GROUPS,)),
            dma((X,)),
            dma((X,)),
            dma((CORES * Z,)),
            dma((CORES * Z,)),
        ],
        compiler_params=pltpu.CompilerParams(
            collective_id=0, has_side_effects=True, vmem_limit_bytes=61 * 1024 * 1024
        ),
    )(field, coefficient, table, transfer)


def solution(mesh):
    placed = (P("freq", None, "seabed", None), P("seabed", None), P("freq", None, None, "seabed"))
    return jax.shard_map(
        shards,
        mesh=mesh,
        in_specs=placed,
        out_specs=P("seabed", "freq", None, None),
        check_vma=False,
    )
```

```python
import functools
import math

import jax
import jax.numpy as jnp
import numpy as np
from jax import lax
from jax.experimental import pallas as pl
from jax.experimental.pallas import tpu as pltpu
from jax.sharding import PartitionSpec as P

MESH = pl.DeviceIdType.MESH
PASSES = 3
CORES = 2
Z = 4
GROUPS = 4
AHEAD = 16
F32 = jnp.float32
BF16 = jnp.bfloat16


def split(value):
    high = value.astype(BF16)
    return high, (value - high.astype(F32)).astype(BF16)


def dot_nt(a, b):
    return lax.dot_general(a, b, (((1,), (1,)), ((), ())), preferred_element_type=F32)


def block_table(vectors, steps, freqs):
    phase = (np.arange(freqs)[:, None] * np.arange(steps)[None, :] % steps) * (2.0 * math.pi / steps)
    table = np.stack([np.cos(phase), -np.sin(phase)], 1) / math.sqrt(steps)
    wide = np.einsum("kbt,vw->kbvwt", table, np.eye(vectors))
    wide = wide.reshape(2 * freqs * vectors, vectors * steps).astype(np.float32)
    high = wide.astype(BF16)
    low = (wide - high.astype(np.float32)).astype(BF16)
    return np.stack([high, low])


def kernel(
    dims, x_hbm, coef_hbm, table_hbm, transfer_ref, out_ref,
    x_ref, coef_ref, table_ref, ext, coefs, outgoing, incoming, raw, t_high, t_low, parts, prod, pair, x_out, x_in, z_out, z_in,
    in_sems, raw_sem, coef_sems, halo_send, halo_recv, a2a_send, a2a_recv, pair_send, pair_recv, x_send, x_recv, z_send, z_recv,
):
    X, F, vectors, steps, rows, width, sens, sens_pad = dims
    size = F // GROUPS
    block_rows = size * vectors
    strips = X * Z * CORES
    s = lax.axis_index("seabed")
    f = lax.axis_index("freq")
    core = s % CORES
    z = (s // CORES) % Z
    x = s // (CORES * Z)
    group_at = x * (CORES * Z)
    local = s % (CORES * Z)
    has_low = s > 0
    has_high = s < strips - 1
    crosses_low = (local == 0) & has_low
    crosses_high = (local == CORES * Z - 1) & has_high

    def x_peer(step):
        return (x + step) % X

    def x_device(at):
        return ((at * Z + z) * CORES + core, f)

    def z_device(at):
        return (group_at + at, f)

    first = [
        pltpu.make_async_copy(source, target, in_sems.at[i])
        for i, (source, target) in enumerate(((x_hbm, x_ref), (table_hbm, table_ref), (coef_hbm, coef_ref)))
    ]
    for copy in first:
        copy.start()
    fetch = [pltpu.make_async_copy(transfer_ref.at[0, a], raw.at[a, pl.ds(0, sens)], raw_sem.at[a]) for a in range(2)]

    barrier = pltpu.get_barrier_semaphore()

    @pl.when(crosses_low)
    def _():
        pl.semaphore_signal(barrier, inc=1, device_id=(s - 1, f), device_id_type=MESH)

    @pl.when(crosses_high)
    def _():
        pl.semaphore_signal(barrier, inc=1, device_id=(s + 1, f), device_id_type=MESH)

    @pl.loop(1, F)
    def _(step):
        pl.semaphore_signal(barrier, inc=1, device_id=(s, (f + step) % F), device_id_type=MESH)

    @pl.loop(1, X)
    def _(step):
        pl.semaphore_signal(barrier, inc=1, device_id=x_device(x_peer(step)), device_id_type=MESH)

    @pl.loop(1, CORES * Z)
    def _(step):
        pl.semaphore_signal(barrier, inc=1, device_id=z_device((local + step) % (CORES * Z)), device_id_type=MESH)

    for copy in fetch:
        copy.start()
    for copy in first:
        copy.wait()

    for r in range(rows):
        block = x_ref[:, r].reshape(vectors * steps, width)
        ext[PASSES + r] = jnp.dot(table_ref[0], block, preferred_element_type=F32) + jnp.dot(
            table_ref[1], block, preferred_element_type=F32
        )
        coefs[PASSES + r] = jnp.broadcast_to(coef_ref[pl.ds(r, 1), :], (8, width))
    raw[:, pl.ds(sens, sens_pad - sens)] = jnp.zeros((2, sens_pad - sens, raw.shape[2]), F32)

    peers = (F - 1) + (X - 1) + (CORES * Z - 1)
    crosses = crosses_low | crosses_high

    @pl.when(crosses)
    def _():
        pl.semaphore_wait(barrier, peers + 1)

    @pl.when(jnp.logical_not(crosses))
    def _():
        pl.semaphore_wait(barrier, peers)

    lines = 2 * vectors
    LOW, HIGH = 0, 1

    def target_of(step):
        g, i = step // size, step % size
        return (f // GROUPS + i) % size * GROUPS + (f % GROUPS + g + i) % GROUPS

    def source_of(g, i):
        return (f // GROUPS + size - i) % size * GROUPS + (f % GROUPS + 2 * F - g - i) % GROUPS

    def coef_copy(side):
        source = coefs.at[pl.ds(rows, PASSES)] if side == LOW else coefs.at[pl.ds(PASSES, PASSES)]
        target = coefs.at[pl.ds(0, PASSES)] if side == LOW else coefs.at[pl.ds(PASSES + rows, PASSES)]
        peer = s + 1 if side == LOW else s - 1
        return pltpu.make_async_remote_copy(
            src_ref=source, dst_ref=target, send_sem=coef_sems.at[side], recv_sem=coef_sems.at[2 + side],
            device_id=(peer, f), device_id_type=MESH,
        )

    def halo_copy(side, step):
        at = pl.ds(pl.multiple_of(target_of(step) * lines, lines), lines)
        source = ext.at[pl.ds(rows, PASSES), at] if side == LOW else ext.at[pl.ds(PASSES, PASSES), at]
        target = ext.at[pl.ds(0, PASSES), at] if side == LOW else ext.at[pl.ds(PASSES + rows, PASSES), at]
        peer = s + 1 if side == LOW else s - 1
        return pltpu.make_async_remote_copy(
            src_ref=source, dst_ref=target, send_sem=halo_send.at[side, step], recv_sem=halo_recv.at[side, step],
            device_id=(peer, f), device_id_type=MESH,
        )

    def halo_start(step):
        @pl.when(has_high)
        def _():
            halo_copy(LOW, step).start()

        @pl.when(has_low)
        def _():
            halo_copy(HIGH, step).start()

    @pl.when(has_high)
    def _():
        coef_copy(LOW).start()

    @pl.when(has_low)
    def _():
        coef_copy(HIGH).start()

    @pl.loop(0, min(AHEAD, F))
    def _(step):
        halo_start(step)

    @pl.when(jnp.logical_not(has_low))
    def _():
        ext[pl.ds(0, PASSES)] = jnp.zeros((PASSES,) + ext.shape[1:], F32)
        coefs[pl.ds(0, PASSES)] = jnp.zeros((PASSES, 8, width), F32)

    @pl.when(jnp.logical_not(has_high))
    def _():
        ext[pl.ds(PASSES + rows, PASSES)] = jnp.zeros((PASSES,) + ext.shape[1:], F32)
        coefs[pl.ds(PASSES + rows, PASSES)] = jnp.zeros((PASSES, 8, width), F32)

    for copy in fetch:
        copy.wait()
    cells = rows * width
    part = 32

    @pl.loop(0, sens_pad // part)
    def _(i):
        at = pl.ds(pl.multiple_of(i * part, part), part)
        for a in range(2):
            high, low = split(raw[a, at])
            t_high[at, pl.ds(a * cells, cells)] = high
            t_low[at, pl.ds(a * cells, cells)] = low

    @pl.when(has_low)
    def _():
        coef_copy(LOW).wait_recv()

    @pl.when(has_high)
    def _():
        coef_copy(HIGH).wait_recv()

    lane = lax.broadcasted_iota(jnp.int32, (8, width), 1)

    def smoothed(at):
        u = [ext[r, at] for r in range(rows + 2 * PASSES)]
        for p in range(PASSES):
            later = []
            for r in range(1, len(u) - 1):
                left = jnp.where(lane == 0, 0.0, pltpu.roll(u[r], 1, 1))
                right = jnp.where(lane == width - 1, 0.0, pltpu.roll(u[r], width - 1, 1))
                beside = (u[r + 1] + u[r - 1]) + (left + right)
                later.append(u[r] + coefs[r + p] * (beside - 4.0 * u[r]))
            u = later
        return u

    def a2a_copy(k, source):
        return pltpu.make_async_remote_copy(
            src_ref=outgoing.at[k], dst_ref=incoming.at[source], send_sem=a2a_send.at[k], recv_sem=a2a_recv.at[source],
            device_id=(s, k), device_id_type=MESH,
        )

    @pl.loop(0, F)
    def _(step):
        @pl.when(has_low)
        def _():
            halo_copy(LOW, step).wait_recv()

        @pl.when(has_high)
        def _():
            halo_copy(HIGH, step).wait_recv()

        @pl.when(step + AHEAD < F)
        def _():
            halo_start(step + AHEAD)

        k = target_of(step)
        for b in range(2):
            at = pl.ds(pl.multiple_of(k * lines + b * vectors, 8), 8)
            for r, value in enumerate(smoothed(at)):
                outgoing[k, b, r] = value

        @pl.when(k != f)
        def _():
            a2a_copy(k, f).start()

        @pl.when(k == f)
        def _():
            incoming[f] = outgoing[f]

    other = 1 - core

    def pair_copy(g):
        return pltpu.make_async_remote_copy(
            src_ref=prod.at[g, other], dst_ref=pair.at[g], send_sem=pair_send.at[g], recv_sem=pair_recv.at[g],
            device_id=(group_at + z * CORES + other, f), device_id_type=MESH,
        )

    def products(g):
        for i in range(size):
            at = source_of(g, i)

            @pl.when(at != f)
            def _():
                pltpu.make_async_remote_copy(
                    src_ref=outgoing.at[at], dst_ref=incoming.at[at], send_sem=a2a_send.at[at],
                    recv_sem=a2a_recv.at[at], device_id=(s, at), device_id_type=MESH,
                ).wait_recv()

        for q in range(size // 2):
            here = pl.ds(q * 16, 16)
            one, two = source_of(g, 2 * q), source_of(g, 2 * q + 1)
            for r in range(rows):
                real = split(jnp.concatenate([incoming[one, 0, r], incoming[two, 0, r]], axis=0))
                imag = split(jnp.concatenate([incoming[one, 1, r], incoming[two, 1, r]], axis=0))
                for i in range(2):
                    parts[i, 0, here, pl.ds(r * width, width)] = real[i]
                    parts[i, 0, here, pl.ds(cells + r * width, width)] = -imag[i]
                    parts[i, 1, here, pl.ds(r * width, width)] = imag[i]
                    parts[i, 1, here, pl.ds(cells + r * width, width)] = real[i]
        both = parts[...].reshape(4 * block_rows, 2 * cells)
        for first in range(0, sens_pad, 256):
            at = pl.ds(first, min(256, sens_pad - first))
            all_high = dot_nt(both, t_high[at])
            total = all_high[: 2 * block_rows] + all_high[2 * block_rows :]
            total += dot_nt(both[: 2 * block_rows], t_low[at])
            prod[g, 0, :, at] = total[:block_rows]
            prod[g, 1, :, at] = total[block_rows:]
        pair_copy(g).start()

    def x_copy(g, i, to, source, half):
        return pltpu.make_async_remote_copy(
            src_ref=x_out.at[g, i], dst_ref=x_in.at[source, half], send_sem=x_send.at[g, i],
            recv_sem=x_recv.at[source, half], device_id=x_device(to), device_id_type=MESH,
        )

    def pass_on(g):
        pair_copy(g).wait_recv()
        for i in range(size):
            to, half = source_of(g, i) // 2, source_of(g, i) % 2
            at = pl.ds(i * vectors, vectors)
            x_out[g, i] = prod[g, core, at] + pair[g, at]

            @pl.when(to != x)
            def _():
                x_copy(g, i, to, x, half).start()

            @pl.when(to == x)
            def _():
                x_in[x, half] = x_out[g, i]

    @pl.loop(0, GROUPS)
    def _(g):
        products(g)

        @pl.when(g > 0)
        def _():
            pass_on(g - 1)

    pass_on(GROUPS - 1)

    @pl.when(has_high)
    def _():
        coef_copy(LOW).wait_send()

    @pl.when(has_low)
    def _():
        coef_copy(HIGH).wait_send()

    @pl.loop(0, F)
    def _(step):
        @pl.when(has_high)
        def _():
            halo_copy(LOW, step).wait_send()

        @pl.when(has_low)
        def _():
            halo_copy(HIGH, step).wait_send()

    @pl.loop(1, F)
    def _(step):
        a2a_copy((f + step) % F, f).wait_send()

    @pl.loop(0, GROUPS)
    def _(g):
        pair_copy(g).wait_send()

    for half in range(2):
        total = x_in[x, half]
        for step in range(1, X):
            source = x_peer(step)
            x_copy(0, 0, source, source, half).wait_recv()
            total += x_in[source, half]
        for at in range(vectors // 2):
            z_out[half * (vectors // 2) + at] = total[2 * at : 2 * at + 2]

    def z_copy(to, source):
        return pltpu.make_async_remote_copy(
            src_ref=z_out.at[to], dst_ref=z_in.at[source], send_sem=z_send.at[to], recv_sem=z_recv.at[source],
            device_id=z_device(to), device_id_type=MESH,
        )

    @pl.loop(1, CORES * Z)
    def _(step):
        z_copy((local + step) % (CORES * Z), local).start()

    z_in[local] = z_out[local]

    for g in range(GROUPS):
        for i in range(size):
            to = source_of(g, i) // 2

            @pl.when(to != x)
            def _():
                x_copy(g, i, to, x, 0).wait_send()

    @pl.loop(1, CORES * Z)
    def _(step):
        source = (local + step) % (CORES * Z)
        z_copy(source, source).wait_recv()

    for part_at in range(2):
        result = z_in[part_at]
        for at in range(1, Z):
            result += z_in[at * CORES + part_at]
        for v in range(2):
            out_ref[v, 0, pl.ds(part_at, 1)] = result[v : v + 1, :sens]

    @pl.loop(1, CORES * Z)
    def _(step):
        z_copy((local + step) % (CORES * Z), local).wait_send()


def shards(uplift, coefficient, transfer):
    vectors, steps, rows, width = uplift.shape
    sens = transfer.shape[2]
    F = lax.axis_size("freq")
    strips = lax.axis_size("seabed")
    X = strips // (Z * CORES)
    all_vectors = vectors * F
    sens_pad = -(-sens // 128) * 128
    cells = rows * width
    dims = (X, F, vectors, steps, rows, width, sens, sens_pad)
    table = jnp.asarray(block_table(vectors, steps, F))
    field = jnp.transpose(uplift, (0, 2, 1, 3))
    dma = pltpu.SemaphoreType.DMA
    vmem = pl.BlockSpec(memory_space=pltpu.VMEM)
    return pl.pallas_call(
        functools.partial(kernel, dims),
        out_shape=jax.ShapeDtypeStruct((2, 1, 2, sens), F32),
        in_specs=[pl.BlockSpec(memory_space=pltpu.HBM)] * 4,
        out_specs=vmem,
        scratch_shapes=[
            pltpu.VMEM((vectors, rows, steps, width), BF16),
            pltpu.VMEM((rows, width), F32),
            pltpu.VMEM(table.shape, BF16),
            pltpu.VMEM((rows + 2 * PASSES, 2 * F * vectors, width), F32),
            pltpu.VMEM((rows + 2 * PASSES, 8, width), F32),
            pltpu.VMEM((F, 2, rows, vectors, width), F32),
            pltpu.VMEM((F, 2, rows, vectors, width), F32),
            pltpu.VMEM((2, sens_pad, cells), F32),
            pltpu.VMEM((sens_pad, 2 * cells), BF16),
            pltpu.VMEM((sens_pad, 2 * cells), BF16),
            pltpu.VMEM((2, 2, all_vectors // GROUPS, 2 * cells), BF16),
            pltpu.VMEM((GROUPS, 2, all_vectors // GROUPS, sens_pad), F32),
            pltpu.VMEM((GROUPS, all_vectors // GROUPS, sens_pad), F32),
            pltpu.VMEM((GROUPS, F // GROUPS, vectors, sens_pad), F32),
            pltpu.VMEM((X, 2, vectors, sens_pad), F32),
            pltpu.VMEM((CORES * Z, 2, sens_pad), F32),
            pltpu.VMEM((CORES * Z, 2, sens_pad), F32),
            dma((3,)),
            dma((2,)),
            dma((4,)),
            dma((2, F)),
            dma((2, F)),
            dma((F,)),
            dma((F,)),
            dma((GROUPS,)),
            dma((GROUPS,)),
            dma((GROUPS, F // GROUPS)),
            dma((X, 2)),
            dma((CORES * Z,)),
            dma((CORES * Z,)),
        ],
        compiler_params=pltpu.CompilerParams(
            collective_id=0, has_side_effects=True, vmem_limit_bytes=61 * 1024 * 1024
        ),
    )(field, coefficient, table, transfer)


def solution(mesh):
    placed = (P("freq", None, "seabed", None), P("seabed", None), P("freq", None, None, "seabed"))
    return jax.shard_map(
        shards,
        mesh=mesh,
        in_specs=placed,
        out_specs=P("seabed", "freq", None, None),
        check_vma=False,
    )
```

```python
import functools
import math

import jax
import jax.numpy as jnp
import numpy as np
from jax import lax
from jax.experimental import pallas as pl
from jax.experimental.pallas import tpu as pltpu
from jax.sharding import PartitionSpec as P

MESH = pl.DeviceIdType.MESH
PASSES = 3
CORES = 2
Z = 4
GROUPS = 4
AHEAD = 16
WINDOW = 8
F32 = jnp.float32
BF16 = jnp.bfloat16


def split(value):
    high = value.astype(BF16)
    return high, (value - high.astype(F32)).astype(BF16)


def dot_nt(a, b):
    return lax.dot_general(a, b, (((1,), (1,)), ((), ())), preferred_element_type=F32)


def block_table(vectors, steps, freqs):
    phase = (np.arange(freqs)[:, None] * np.arange(steps)[None, :] % steps) * (2.0 * math.pi / steps)
    table = np.stack([np.cos(phase), -np.sin(phase)], 1) / math.sqrt(steps)
    wide = np.einsum("kbt,vw->kbvwt", table, np.eye(vectors))
    wide = wide.reshape(2 * freqs * vectors, vectors * steps).astype(np.float32)
    high = wide.astype(BF16)
    low = (wide - high.astype(np.float32)).astype(BF16)
    return np.stack([high, low])


def kernel(
    dims, x_hbm, coef_hbm, table_hbm, transfer_ref, out_ref,
    x_ref, coef_ref, table_ref, ext, coefs, outgoing, incoming, raw, t_high, t_low, parts, prod, pair, x_out, x_in, z_out, z_in,
    in_sems, raw_sem, coef_sems, halo_send, halo_recv, a2a_send, a2a_recv, pair_send, pair_recv, x_send, x_recv, z_send, z_recv,
):
    X, F, vectors, steps, rows, width, sens, sens_pad = dims
    size = F // GROUPS
    block_rows = size * vectors
    strips = X * Z * CORES
    s = lax.axis_index("seabed")
    f = lax.axis_index("freq")
    core = s % CORES
    z = (s // CORES) % Z
    x = s // (CORES * Z)
    group_at = x * (CORES * Z)
    local = s % (CORES * Z)
    has_low = s > 0
    has_high = s < strips - 1
    crosses_low = (local == 0) & has_low
    crosses_high = (local == CORES * Z - 1) & has_high

    def x_peer(step):
        return (x + step) % X

    def x_device(at):
        return ((at * Z + z) * CORES + core, f)

    def z_device(at):
        return (group_at + at, f)

    first = [
        pltpu.make_async_copy(source, target, in_sems.at[i])
        for i, (source, target) in enumerate(((x_hbm, x_ref), (table_hbm, table_ref), (coef_hbm, coef_ref)))
    ]
    for copy in first:
        copy.start()
    fetch = [pltpu.make_async_copy(transfer_ref.at[0, a], raw.at[a, pl.ds(0, sens)], raw_sem.at[a]) for a in range(2)]

    barrier = pltpu.get_barrier_semaphore()

    @pl.when(crosses_low)
    def _():
        pl.semaphore_signal(barrier, inc=1, device_id=(s - 1, f), device_id_type=MESH)

    @pl.when(crosses_high)
    def _():
        pl.semaphore_signal(barrier, inc=1, device_id=(s + 1, f), device_id_type=MESH)

    @pl.loop(1, F)
    def _(step):
        pl.semaphore_signal(barrier, inc=1, device_id=(s, (f + step) % F), device_id_type=MESH)

    @pl.loop(1, X)
    def _(step):
        pl.semaphore_signal(barrier, inc=1, device_id=x_device(x_peer(step)), device_id_type=MESH)

    @pl.loop(1, CORES * Z)
    def _(step):
        pl.semaphore_signal(barrier, inc=1, device_id=z_device((local + step) % (CORES * Z)), device_id_type=MESH)

    for copy in fetch:
        copy.start()
    for copy in first:
        copy.wait()

    for r in range(rows):
        block = x_ref[:, r].reshape(vectors * steps, width)
        ext[PASSES + r] = jnp.dot(table_ref[0], block, preferred_element_type=F32) + jnp.dot(
            table_ref[1], block, preferred_element_type=F32
        )
        coefs[PASSES + r] = jnp.broadcast_to(coef_ref[pl.ds(r, 1), :], (8, width))
    raw[:, pl.ds(sens, sens_pad - sens)] = jnp.zeros((2, sens_pad - sens, raw.shape[2]), F32)

    peers = (F - 1) + (X - 1) + (CORES * Z - 1)
    crosses = crosses_low | crosses_high

    @pl.when(crosses)
    def _():
        pl.semaphore_wait(barrier, peers + 1)

    @pl.when(jnp.logical_not(crosses))
    def _():
        pl.semaphore_wait(barrier, peers)

    lines = 2 * vectors
    LOW, HIGH = 0, 1

    def target_of(step):
        g, i = step // size, step % size
        return (f // GROUPS + i) % size * GROUPS + (f % GROUPS + g + i) % GROUPS

    def source_of(g, i):
        return (f // GROUPS + size - i) % size * GROUPS + (f % GROUPS + 2 * F - g - i) % GROUPS

    def coef_copy(side):
        source = coefs.at[pl.ds(rows, PASSES)] if side == LOW else coefs.at[pl.ds(PASSES, PASSES)]
        target = coefs.at[pl.ds(0, PASSES)] if side == LOW else coefs.at[pl.ds(PASSES + rows, PASSES)]
        peer = s + 1 if side == LOW else s - 1
        return pltpu.make_async_remote_copy(
            src_ref=source, dst_ref=target, send_sem=coef_sems.at[side], recv_sem=coef_sems.at[2 + side],
            device_id=(peer, f), device_id_type=MESH,
        )

    def halo_copy(side, step):
        at = pl.ds(pl.multiple_of(target_of(step) * lines, lines), lines)
        source = ext.at[pl.ds(rows, PASSES), at] if side == LOW else ext.at[pl.ds(PASSES, PASSES), at]
        target = ext.at[pl.ds(0, PASSES), at] if side == LOW else ext.at[pl.ds(PASSES + rows, PASSES), at]
        peer = s + 1 if side == LOW else s - 1
        return pltpu.make_async_remote_copy(
            src_ref=source, dst_ref=target, send_sem=halo_send.at[side, step], recv_sem=halo_recv.at[side, step],
            device_id=(peer, f), device_id_type=MESH,
        )

    def halo_start(step):
        @pl.when(has_high)
        def _():
            halo_copy(LOW, step).start()

        @pl.when(has_low)
        def _():
            halo_copy(HIGH, step).start()

    @pl.when(has_high)
    def _():
        coef_copy(LOW).start()

    @pl.when(has_low)
    def _():
        coef_copy(HIGH).start()

    @pl.loop(0, min(AHEAD, F))
    def _(step):
        halo_start(step)

    @pl.when(jnp.logical_not(has_low))
    def _():
        ext[pl.ds(0, PASSES)] = jnp.zeros((PASSES,) + ext.shape[1:], F32)
        coefs[pl.ds(0, PASSES)] = jnp.zeros((PASSES, 8, width), F32)

    @pl.when(jnp.logical_not(has_high))
    def _():
        ext[pl.ds(PASSES + rows, PASSES)] = jnp.zeros((PASSES,) + ext.shape[1:], F32)
        coefs[pl.ds(PASSES + rows, PASSES)] = jnp.zeros((PASSES, 8, width), F32)

    for copy in fetch:
        copy.wait()
    cells = rows * width
    part = 32

    @pl.loop(0, sens_pad // part)
    def _(i):
        at = pl.ds(pl.multiple_of(i * part, part), part)
        for a in range(2):
            high, low = split(raw[a, at])
            t_high[at, pl.ds(a * cells, cells)] = high
            t_low[at, pl.ds(a * cells, cells)] = low

    @pl.when(has_low)
    def _():
        coef_copy(LOW).wait_recv()

    @pl.when(has_high)
    def _():
        coef_copy(HIGH).wait_recv()

    lane = lax.broadcasted_iota(jnp.int32, (8, width), 1)

    def smoothed(at):
        u = [ext[r, at] for r in range(rows + 2 * PASSES)]
        for p in range(PASSES):
            later = []
            for r in range(1, len(u) - 1):
                left = jnp.where(lane == 0, 0.0, pltpu.roll(u[r], 1, 1))
                right = jnp.where(lane == width - 1, 0.0, pltpu.roll(u[r], width - 1, 1))
                beside = (u[r + 1] + u[r - 1]) + (left + right)
                later.append(u[r] + coefs[r + p] * (beside - 4.0 * u[r]))
            u = later
        return u

    def a2a_copy(k, source):
        return pltpu.make_async_remote_copy(
            src_ref=outgoing.at[k], dst_ref=incoming.at[source], send_sem=a2a_send.at[k], recv_sem=a2a_recv.at[source],
            device_id=(s, k), device_id_type=MESH,
        )

    def a2a_left(step):
        k = target_of(step)

        @pl.when(k != f)
        def _():
            a2a_copy(k, f).wait_send()

    @pl.loop(0, F)
    def _(step):
        @pl.when(has_low)
        def _():
            halo_copy(LOW, step).wait_recv()

        @pl.when(has_high)
        def _():
            halo_copy(HIGH, step).wait_recv()

        @pl.when(step + AHEAD < F)
        def _():
            halo_start(step + AHEAD)

        k = target_of(step)
        for b in range(2):
            at = pl.ds(pl.multiple_of(k * lines + b * vectors, 8), 8)
            for r, value in enumerate(smoothed(at)):
                outgoing[k, b, r] = value

        @pl.when(step >= WINDOW)
        def _():
            a2a_left(step - WINDOW)

        @pl.when(k != f)
        def _():
            a2a_copy(k, f).start()

        @pl.when(k == f)
        def _():
            incoming[f] = outgoing[f]

    other = 1 - core

    def pair_copy(g):
        return pltpu.make_async_remote_copy(
            src_ref=prod.at[g, other], dst_ref=pair.at[g], send_sem=pair_send.at[g], recv_sem=pair_recv.at[g],
            device_id=(group_at + z * CORES + other, f), device_id_type=MESH,
        )

    def products(g):
        for i in range(size):
            at = source_of(g, i)

            @pl.when(at != f)
            def _():
                pltpu.make_async_remote_copy(
                    src_ref=outgoing.at[at], dst_ref=incoming.at[at], send_sem=a2a_send.at[at],
                    recv_sem=a2a_recv.at[at], device_id=(s, at), device_id_type=MESH,
                ).wait_recv()

        for q in range(size // 2):
            here = pl.ds(q * 16, 16)
            one, two = source_of(g, 2 * q), source_of(g, 2 * q + 1)
            for r in range(rows):
                real = split(jnp.concatenate([incoming[one, 0, r], incoming[two, 0, r]], axis=0))
                imag = split(jnp.concatenate([incoming[one, 1, r], incoming[two, 1, r]], axis=0))
                for i in range(2):
                    parts[i, 0, here, pl.ds(r * width, width)] = real[i]
                    parts[i, 0, here, pl.ds(cells + r * width, width)] = -imag[i]
                    parts[i, 1, here, pl.ds(r * width, width)] = imag[i]
                    parts[i, 1, here, pl.ds(cells + r * width, width)] = real[i]
        both = parts[...].reshape(4 * block_rows, 2 * cells)
        for first in range(0, sens_pad, 256):
            at = pl.ds(first, min(256, sens_pad - first))
            all_high = dot_nt(both, t_high[at])
            total = all_high[: 2 * block_rows] + all_high[2 * block_rows :]
            total += dot_nt(both[: 2 * block_rows], t_low[at])
            prod[g, 0, :, at] = total[:block_rows]
            prod[g, 1, :, at] = total[block_rows:]
        pair_copy(g).start()

    def x_copy(g, i, to, source, half):
        return pltpu.make_async_remote_copy(
            src_ref=x_out.at[g, i], dst_ref=x_in.at[source, half], send_sem=x_send.at[g, i],
            recv_sem=x_recv.at[source, half], device_id=x_device(to), device_id_type=MESH,
        )

    def pass_on(g):
        pair_copy(g).wait_recv()
        for i in range(size):
            to, half = source_of(g, i) // 2, source_of(g, i) % 2
            at = pl.ds(i * vectors, vectors)
            x_out[g, i] = prod[g, core, at] + pair[g, at]

            @pl.when(to != x)
            def _():
                x_copy(g, i, to, x, half).start()

            @pl.when(to == x)
            def _():
                x_in[x, half] = x_out[g, i]

    @pl.loop(0, GROUPS)
    def _(g):
        products(g)

        @pl.when(g > 0)
        def _():
            pass_on(g - 1)

    pass_on(GROUPS - 1)

    @pl.when(has_high)
    def _():
        coef_copy(LOW).wait_send()

    @pl.when(has_low)
    def _():
        coef_copy(HIGH).wait_send()

    @pl.loop(0, F)
    def _(step):
        @pl.when(has_high)
        def _():
            halo_copy(LOW, step).wait_send()

        @pl.when(has_low)
        def _():
            halo_copy(HIGH, step).wait_send()

    @pl.loop(F - WINDOW, F)
    def _(step):
        a2a_left(step)

    @pl.loop(0, GROUPS)
    def _(g):
        pair_copy(g).wait_send()

    for half in range(2):
        total = x_in[x, half]
        for step in range(1, X):
            source = x_peer(step)
            x_copy(0, 0, source, source, half).wait_recv()
            total += x_in[source, half]
        for at in range(vectors // 2):
            z_out[half * (vectors // 2) + at] = total[2 * at : 2 * at + 2]

    def z_copy(to, source):
        return pltpu.make_async_remote_copy(
            src_ref=z_out.at[to], dst_ref=z_in.at[source], send_sem=z_send.at[to], recv_sem=z_recv.at[source],
            device_id=z_device(to), device_id_type=MESH,
        )

    @pl.loop(1, CORES * Z)
    def _(step):
        z_copy((local + step) % (CORES * Z), local).start()

    z_in[local] = z_out[local]

    for g in range(GROUPS):
        for i in range(size):
            to = source_of(g, i) // 2

            @pl.when(to != x)
            def _():
                x_copy(g, i, to, x, 0).wait_send()

    @pl.loop(1, CORES * Z)
    def _(step):
        source = (local + step) % (CORES * Z)
        z_copy(source, source).wait_recv()

    for part_at in range(2):
        result = z_in[part_at]
        for at in range(1, Z):
            result += z_in[at * CORES + part_at]
        for v in range(2):
            out_ref[v, 0, pl.ds(part_at, 1)] = result[v : v + 1, :sens]

    @pl.loop(1, CORES * Z)
    def _(step):
        z_copy((local + step) % (CORES * Z), local).wait_send()


def shards(uplift, coefficient, transfer):
    vectors, steps, rows, width = uplift.shape
    sens = transfer.shape[2]
    F = lax.axis_size("freq")
    strips = lax.axis_size("seabed")
    X = strips // (Z * CORES)
    all_vectors = vectors * F
    sens_pad = -(-sens // 128) * 128
    cells = rows * width
    dims = (X, F, vectors, steps, rows, width, sens, sens_pad)
    table = jnp.asarray(block_table(vectors, steps, F))
    field = jnp.transpose(uplift, (0, 2, 1, 3))
    dma = pltpu.SemaphoreType.DMA
    vmem = pl.BlockSpec(memory_space=pltpu.VMEM)
    return pl.pallas_call(
        functools.partial(kernel, dims),
        out_shape=jax.ShapeDtypeStruct((2, 1, 2, sens), F32),
        in_specs=[pl.BlockSpec(memory_space=pltpu.HBM)] * 4,
        out_specs=vmem,
        scratch_shapes=[
            pltpu.VMEM((vectors, rows, steps, width), BF16),
            pltpu.VMEM((rows, width), F32),
            pltpu.VMEM(table.shape, BF16),
            pltpu.VMEM((rows + 2 * PASSES, 2 * F * vectors, width), F32),
            pltpu.VMEM((rows + 2 * PASSES, 8, width), F32),
            pltpu.VMEM((F, 2, rows, vectors, width), F32),
            pltpu.VMEM((F, 2, rows, vectors, width), F32),
            pltpu.VMEM((2, sens_pad, cells), F32),
            pltpu.VMEM((sens_pad, 2 * cells), BF16),
            pltpu.VMEM((sens_pad, 2 * cells), BF16),
            pltpu.VMEM((2, 2, all_vectors // GROUPS, 2 * cells), BF16),
            pltpu.VMEM((GROUPS, 2, all_vectors // GROUPS, sens_pad), F32),
            pltpu.VMEM((GROUPS, all_vectors // GROUPS, sens_pad), F32),
            pltpu.VMEM((GROUPS, F // GROUPS, vectors, sens_pad), F32),
            pltpu.VMEM((X, 2, vectors, sens_pad), F32),
            pltpu.VMEM((CORES * Z, 2, sens_pad), F32),
            pltpu.VMEM((CORES * Z, 2, sens_pad), F32),
            dma((3,)),
            dma((2,)),
            dma((4,)),
            dma((2, F)),
            dma((2, F)),
            dma((F,)),
            dma((F,)),
            dma((GROUPS,)),
            dma((GROUPS,)),
            dma((GROUPS, F // GROUPS)),
            dma((X, 2)),
            dma((CORES * Z,)),
            dma((CORES * Z,)),
        ],
        compiler_params=pltpu.CompilerParams(
            collective_id=0, has_side_effects=True, vmem_limit_bytes=61 * 1024 * 1024
        ),
    )(field, coefficient, table, transfer)


def solution(mesh):
    placed = (P("freq", None, "seabed", None), P("seabed", None), P("freq", None, None, "seabed"))
    return jax.shard_map(
        shards,
        mesh=mesh,
        in_specs=placed,
        out_specs=P("seabed", "freq", None, None),
        check_vma=False,
    )
```
